512 devices in a mesh: tm: 16 (over y, core), space: 32 (over x, z).
Axes of the slice: x: 4, y: 8, z: 8, core: 2. Of those that a mesh axis runs over, the one named last changes fastest.
Arguments:
- initial_state: float32 [3, 256, 32, 128], P(None, 'space'), may hold values from -4 to 4
- guess: float32 [16, 3, 256, 32, 128], P('tm', None, 'space'), may hold values from -4 to 4
- soil_kind_index: int32 [256, 32, 128], P('space'), may hold values from 0 to 3
Outputs:
- corrected: float32 [16, 3, 256, 32, 128], P('tm', None, 'space')
- relaxed: float32 [16, 3, 256, 32, 128], P('tm', None, 'space')
The draws below stay inside these ranges and needn't reach their ends.
All inputs are finite; a program needn't handle non-finite values.
Results may differ from the reference program's by a relative error of at most 0.00002.
Values sent between devices are 32-bit elements; how exact they have to be, the bound alone decides.
No kernel may reach another device: no remote copies, remote signals or barrier semaphores. Data moves between devices by JAX's collectives and lax.ppermute only.
A program may use at most 64 MiB of HBM per device.

```python
import jax
import jax.numpy as jnp
from jax import lax

NY = 128
NZ = 32
RATIO = 8
NX = 256
COARSE_POINTS = 16


def set_ends(result, own_key, smallest, largest):
    index_at = [jax.random.randint(jax.random.fold_in(own_key, axis), (), 0, length) for axis, length in enumerate(result.shape)]
    widest = result.shape.index(max(result.shape))
    next_to = index_at[:widest] + [(index_at[widest] + 1) % result.shape[widest]] + index_at[widest + 1:]
    return result.at[tuple(index_at)].set(smallest).at[tuple(next_to)].set(largest)


def block_scale(rng, shape, cuts, low, top_value):
    loudness, own = 1.0, jax.random.fold_in(rng, 6)
    for position, blocks in cuts:
        heights = jnp.exp(jax.random.uniform(jax.random.fold_in(own, position), (blocks,), jnp.float32, low / len(cuts), top_value / len(cuts)))
        loudness = loudness * jnp.repeat(heights, shape[position] // blocks).reshape([-1 if axis == position else 1 for axis in range(len(shape))])
    return loudness


def centred(own_key, shape, scale, limit, shards=(), dtype=jnp.bfloat16):
    factor_of = block_scale(own_key, shape, shards, -0.22, 0.18) if shards else 1.0
    array = jax.random.normal(own_key, shape, jnp.float32) * scale * factor_of
    return jnp.minimum(jnp.maximum(array, -limit), limit).astype(dtype)


def setup_inputs(seed: int = 0) -> dict:
    arg_keys = jax.random.split(jax.random.key(seed), 4)
    return {
        "initial_state": centred(arg_keys[0], (3, NX, NZ, NY), 1.0, 4.0, ((1, 32),), jnp.float32),
        "guess": centred(arg_keys[1], (COARSE_POINTS, 3, NX, NZ, NY), 1.0, 4.0, ((0, 16), (2, 32)), jnp.float32),
        "soil_kind_index": set_ends(jax.random.randint(arg_keys[2], (NX, NZ, NY), 0, 4), jax.random.fold_in(arg_keys[2], 1), 0, 3).astype(jnp.int32),
    }


KAPPA = (0.05, 0.08, 0.12, 0.15)
PORE_DIFF = (0.1, 0.04, 0.15, 0.07)
ENERGY = (0.5, 1.0, 1.5, 2.0)
FLUIDITY = (0.2, 0.35, 0.15, 0.3)
STRENGTH = (1.0, 0.6, 1.4, 0.8)
FRICTION_WARMING = 0.3
DRAINAGE = 0.5
DILATANCY = 0.4
TIME_STEP = 0.02


def lookup(soil_kind_index, table):
    looked = jnp.full(soil_kind_index.shape, table[0], jnp.float32)
    for entry in range(1, len(table)):
        looked = jnp.where(soil_kind_index == entry, jnp.float32(table[entry]), looked)
    return looked


def march_solution(heat_level_map, irreversible_deformation, water_stress, heat_level_curvature, water_stress_curvature, soil_kind_index, forward_euler_update):
    heat_diffusion_map = lookup(soil_kind_index, KAPPA)
    pore_map = lookup(soil_kind_index, PORE_DIFF)
    warmth_content = lookup(soil_kind_index, ENERGY)
    fluidity = lookup(soil_kind_index, FLUIDITY)
    strength = lookup(soil_kind_index, STRENGTH)
    activation_multiplier = jnp.exp(warmth_content * (1.0 - 1.0 / (1.5 + jnp.tanh(heat_level_map))))
    yielding_velocity = fluidity * activation_multiplier * jax.nn.softplus(strength - 0.5 * water_stress)
    next_heat_level = heat_level_map + forward_euler_update * (heat_diffusion_map * heat_level_curvature + FRICTION_WARMING * yielding_velocity)
    next_irreversible_deformation = irreversible_deformation + forward_euler_update * yielding_velocity
    next_water_stress = water_stress + forward_euler_update * (pore_map * water_stress_curvature - DRAINAGE * water_stress - DILATANCY * yielding_velocity)
    return next_heat_level, next_irreversible_deformation, next_water_stress


def box_sum(field, along):
    margins = [(0, 0)] * field.ndim
    margins[along] = (1, 1)
    padded = jnp.pad(field, margins)
    length = field.shape[along]
    return (lax.slice_in_dim(padded, 0, length, axis=along)
            + lax.slice_in_dim(padded, 1, length + 1, axis=along)
            + lax.slice_in_dim(padded, 2, length + 2, axis=along))


def laplace(field):
    return box_sum(box_sum(box_sum(field, 0), 1), 2) - 27.0 * field


def step(fields, soil_kind_index, forward_euler_update):
    new = march_solution(fields[0], fields[1], fields[2], laplace(fields[0]), laplace(fields[2]), soil_kind_index, forward_euler_update)
    return jnp.stack(new, 0)


def advance(fields, soil_kind_index, nsteps, forward_euler_update):
    return lax.fori_loop(0, nsteps, lambda turn, current: step(current, soil_kind_index, forward_euler_update), fields)


def reference(initial_state, guess, soil_kind_index):
    coarse_dt = RATIO * TIME_STEP
    starts = jnp.concatenate([initial_state[None], guess[:-1]], 0)
    relaxed = lax.map(lambda fields: advance(fields, soil_kind_index, RATIO, TIME_STEP), starts)
    second = jnp.concatenate([initial_state[None], relaxed[:-1]], 0)
    propagated = lax.map(lambda fields: advance(fields, soil_kind_index, RATIO, TIME_STEP), second)
    coarse = lax.map(lambda fields: step(fields, soil_kind_index, coarse_dt), second)
    defect = propagated - coarse

    def chain(current, term):
        following = step(current, soil_kind_index, coarse_dt) + term
        return following, following

    unused, corrected = lax.scan(chain, initial_state, defect)
    return (corrected, relaxed)
```

```python
import functools
import math

import jax
import jax.numpy as jnp
from jax import lax
from jax.experimental import pallas as pl
from jax.experimental.pallas import tpu as pltpu
from jax.sharding import PartitionSpec as P

RATIO = 8
KAPPA = (0.05, 0.08, 0.12, 0.15)
PORE_DIFF = (0.1, 0.04, 0.15, 0.07)
ENERGY = (0.5, 1.0, 1.5, 2.0)
FLUIDITY = (0.2, 0.35, 0.15, 0.3)
STRENGTH = (1.0, 0.6, 1.4, 0.8)
FRICTION_WARMING = 0.3
DRAINAGE = 0.5
DILATANCY = 0.4
TIME_STEP = 0.02
LOG2E = math.log2(math.e)
LN2 = math.log(2.0)

TILE = 8
EXT = 3 * TILE
STEPS_AHEAD = 7
VMEM = functools.partial(pl.BlockSpec, memory_space=pltpu.VMEM)
SMEM = functools.partial(pl.BlockSpec, memory_space=pltpu.SMEM)
F32 = jnp.float32


def load_rows(ref, *at):
    return [ref[(*at, pl.ds(r, 8, stride=4), slice(None))] for r in range(4)]


def store_rows(ref, rows, *at):
    for r in range(4):
        ref[(*at, pl.ds(r, 8, stride=4), slice(None))] = rows[r]


def load4(ref, *at):
    *lead, layer = at
    return [ref[(*lead, layer * 4 + r)] for r in range(4)]


def store4(ref, rows, *at):
    *lead, layer = at
    for r in range(4):
        ref[(*lead, layer * 4 + r)] = rows[r]


def edges():
    lane = lax.broadcasted_iota(jnp.int32, (8, 128), 1)
    sub = lax.broadcasted_iota(jnp.int32, (8, 128), 0)
    return lane == 0, lane == 127, sub == 0, sub == 7


def curvature(below, here, above, ends):
    lane0, lane127, sub0, sub7 = ends
    s = [a + b + c for a, b, c in zip(below, here, above)]
    first, second = s[0] + s[1], s[2] + s[3]
    before = jnp.where(sub0, 0.0, pltpu.roll(s[3], 1, 0))
    after = jnp.where(sub7, 0.0, pltpu.roll(s[0], 7, 0))
    columns = [before + first, first + s[2], s[1] + second, second + after]
    out = []
    for c, v in zip(columns, here):
        left = jnp.where(lane0, 0.0, pltpu.roll(c, 1, 1))
        right = jnp.where(lane127, 0.0, pltpu.roll(c, 127, 1))
        out.append((c + left + right) - 27.0 * v)
    return out


def increments(load, tabs, at, ends):
    here_t, here_w = load(0, 0), load(1, 0)
    curve_t = curvature(load(0, -1), here_t, load(0, 1), ends)
    curve_w = curvature(load(1, -1), here_w, load(1, 1), ends)
    hk, hc, c0, c1, s = (load4(tabs, i, at) for i in range(5))
    inc_t, inc_p, inc_w = [], [], []
    for r in range(4):
        warm = 1.0 / (1.5 + jnp.tanh(here_t[r]))
        x = s[r] - 0.5 * here_w[r]
        soft = jnp.maximum(x, 0.0) + LN2 * jnp.log2(1.0 + jnp.exp2(-LOG2E * jnp.abs(x)))
        flow = jnp.exp2(c0[r] - c1[r] * warm) * soft
        inc_t.append(hk[r] * curve_t[r] + FRICTION_WARMING * flow)
        inc_p.append(flow)
        inc_w.append(hc[r] * curve_w[r] - (DRAINAGE * TIME_STEP) * here_w[r] - DILATANCY * flow)
    return here_t, here_w, inc_t, inc_p, inc_w


def plus(a, b):
    return [x + y for x, y in zip(a, b)]


def make_tables(flag, soils, tabs):
    for part, load in enumerate(soils):
        def one(i, _):
            kinds = load(i)
            out = [[] for _ in range(5)]
            for kind in kinds:
                def pick(table):
                    got = jnp.full((8, 128), table[0], F32)
                    for entry in range(1, 4):
                        got = jnp.where(kind == float(entry), F32(table[entry]), got)
                    return got
                rows = [
                    pick([TIME_STEP * v for v in KAPPA]),
                    pick([TIME_STEP * v for v in PORE_DIFF]),
                    pick([LOG2E * e + math.log2(TIME_STEP * f) for e, f in zip(ENERGY, FLUIDITY)]),
                    pick([LOG2E * e for e in ENERGY]),
                    pick(STRENGTH),
                ]
                if part != 1:
                    inside = flag[0 if part == 0 else 1]
                    rows[0], rows[1], rows[3] = rows[0] * inside, rows[1] * inside, rows[3] * inside
                    rows[2] = rows[2] - 1000.0 * (1.0 - inside)
                for o, v in zip(out, rows):
                    o.append(v)
            for k in range(5):
                store4(tabs, out[k], k, part * TILE + i)
            return 0
        lax.fori_loop(0, TILE, one, 0)


def fine_steps(bufs, tabs, ps, finish, ends, first_extra=None):
    for t in range(RATIO):
        src, dst = bufs[t % 2], bufs[(t + 1) % 2]

        def one(l, _, t=t, src=src, dst=dst, tile=False):
            load = lambda f, d: load4(src, f, l + d)
            here_t, here_w, inc_t, inc_p, inc_w = increments(load, tabs, l, ends)
            new_t, new_w = plus(here_t, inc_t), plus(here_w, inc_w)
            if tile:
                i = l - TILE
                if t == 0:
                    store4(ps, inc_p, i)
                    if first_extra is not None:
                        first_extra(i, here_t, here_w, inc_t, inc_p, inc_w)
                else:
                    store4(ps, plus(load4(ps, i), inc_p), i)
            if t == RATIO - 1:
                finish(l - TILE, new_t, new_w)
            else:
                store4(dst, new_t, 0, l)
                store4(dst, new_w, 1, l)
            return 0

        if t < RATIO - 1:
            lax.fori_loop(1 + t, TILE, one, 0)
        lax.fori_loop(TILE, 2 * TILE, functools.partial(one, tile=True), 0)
        if t < RATIO - 1:
            lax.fori_loop(2 * TILE, EXT - 1 - t, one, 0)


def gather_ext(buf, left, centre, right, fields):
    def one(i, _):
        for f, (a, b, c) in enumerate(fields):
            store4(buf, load_rows(left, a, i), f, i)
            store4(buf, load_rows(centre, b, i), f, TILE + i)
            store4(buf, load_rows(right, c, i), f, 2 * TILE + i)
        return 0
    lax.fori_loop(0, TILE, one, 0)


def relax_kernel(flag, centre, pressure, left, right, soil, out, tabs, a, b, ps):
    ends = edges()
    make_tables(
        flag,
        (
            lambda i: load_rows(left, 2, i),
            lambda i: [k.astype(F32) for k in load_rows(soil, i)],
            lambda i: load_rows(right, 2, i),
        ),
        tabs,
    )
    gather_ext(a, left, centre, right, ((0, 0, 0), (1, 1, 1)))

    def finish(i, theta, w):
        store_rows(out, theta, 0, i)
        store_rows(out, w, 2, i)

    fine_steps((a, b), tabs, ps, finish, ends)

    def strain(i, _):
        store_rows(out, plus(load_rows(pressure, i), load4(ps, i)), 1, i)
        return 0
    lax.fori_loop(0, TILE, strain, 0)


def defect_kernel(flag, centre, left, right, tabs, out, out_p, a, b, ps, coarse):
    ends = edges()
    gather_ext(a, left, centre, right, ((0, 0, 0), (1, 2, 1)))
    later = 1.0 - flag[2]

    def first_extra(i, here_t, here_w, inc_t, inc_p, inc_w):
        store4(coarse, [later * (v + RATIO * d) for v, d in zip(here_t, inc_t)], 0, i)
        store4(coarse, [(later * RATIO) * d for d in inc_p], 1, i)
        store4(coarse, [later * (v + RATIO * d) for v, d in zip(here_w, inc_w)], 2, i)

    def finish(i, theta, w):
        store_rows(out, [v - g for v, g in zip(theta, load4(coarse, 0, i))], 0, i)
        store_rows(out, [v - g for v, g in zip(w, load4(coarse, 2, i))], 1, i)

    fine_steps((a, b), tabs, ps, finish, ends, first_extra)

    def strain(i, _):
        rows = zip(load_rows(centre, 1, i), load4(ps, i), load4(coarse, 1, i))
        store_rows(out_p, [flag[2] * p + (s - g) for p, s, g in rows], i)
        return 0
    lax.fori_loop(0, TILE, strain, 0)


def coarse_kernel(halo, state, tabs, left, centre, right, strain, held, out, out_p, out_held):
    ends = edges()
    new = halo - 1

    def one(o, _, kind=None):
        i = o + 1
        at = TILE - halo + i
        load = lambda f, d: load_rows(state, f, i + d)
        here_t, here_w, inc_t, inc_p, inc_w = increments(load, tabs, at, ends)
        if kind == 0:
            d, j = left, o + STEPS_AHEAD - new
        elif kind == 1:
            d, j = centre, o - new
            store_rows(out_p, [p + RATIO * v for p, v in zip(load_rows(strain, j), inc_p)], j)
            store_rows(out_held, plus(load_rows(held, 0, j), here_t), 0, j)
            store_rows(out_held, plus(load_rows(held, 1, j), here_w), 1, j)
        else:
            d, j = right, o - new - TILE
        store_rows(out, [(v + RATIO * x) + e for v, x, e in zip(here_t, inc_t, load_rows(d, 0, j))], 0, o)
        store_rows(out, [(v + RATIO * x) + e for v, x, e in zip(here_w, inc_w, load_rows(d, 1, j))], 1, o)
        return 0

    if new:
        lax.fori_loop(0, new, functools.partial(one, kind=0), 0)
    lax.fori_loop(new, new + TILE, functools.partial(one, kind=1), 0)
    if new:
        lax.fori_loop(new + TILE, 2 * new + TILE, functools.partial(one, kind=2), 0)


def call(kernel, outs, scratch, n_in, smem_first=True, **kw):
    specs = [VMEM() for _ in range(n_in)]
    if smem_first:
        specs[0] = SMEM()
    return pl.pallas_call(
        kernel,
        out_shape=[jax.ShapeDtypeStruct(s, F32) for s in outs],
        in_specs=specs,
        out_specs=[VMEM() for _ in outs],
        scratch_shapes=[pltpu.VMEM(s, F32) for s in scratch],
        compiler_params=pltpu.CompilerParams(vmem_limit_bytes=24 * 2**20),
        **kw,
    )


LAYER = (32, 128)
REGS = (8, 128)


def on_device(nt, ns, initial_state, guess, soil):
    t, s = lax.axis_index("tm"), lax.axis_index("space")
    flag = jnp.stack([s > 0, s < ns - 1, t == 0]).astype(F32)
    both = ("tm", "space")

    def shifted(x, dt, ds, only=None):
        pairs = []
        for a in range(nt) if only is None else only:
            for b in range(ns):
                if 0 <= b + ds < ns:
                    pairs.append((a * ns + b, (a + dt) % nt * ns + b + ds))
        return lax.ppermute(x, both, pairs)

    mine = jnp.where(t == nt - 1, initial_state, guess[0])
    heat_stress = jnp.stack([mine[0], mine[2]])
    packed = jnp.concatenate([heat_stress, soil.astype(F32)[None]])
    from_left = shifted(packed, 1, 1)
    from_right = shifted(packed, 1, -1)
    centre = shifted(heat_stress, 1, 0)
    pressure = shifted(mine[1], 1, 0)
    relaxed, tabs = call(
        relax_kernel,
        [(3, TILE, *LAYER), (5, EXT * 4, *REGS)],
        [(2, EXT * 4, *REGS), (2, EXT * 4, *REGS), (TILE * 4, *REGS)],
        6,
    )(flag, centre, pressure, from_left, from_right, soil)

    heat_stress = jnp.stack([relaxed[0], relaxed[2]])
    from_left = shifted(heat_stress, 0, 1)
    from_right = shifted(heat_stress, 0, -1)
    defect, strain = call(
        defect_kernel,
        [(2, TILE, *LAYER), (TILE, *LAYER)],
        [(2, EXT * 4, *REGS), (2, EXT * 4, *REGS), (TILE * 4, *REGS), (3, TILE * 4, *REGS)],
        5,
    )(flag, relaxed, from_left, from_right, tabs)

    ahead = STEPS_AHEAD
    left = shifted(defect[:, TILE - ahead:], 0, 1)
    right = shifted(defect[:, :ahead], 0, -1)
    zero = jnp.zeros((), F32)
    held = jnp.where(t == 0, jnp.stack([relaxed[0], relaxed[2]]), zero)
    held_p = jnp.where(t == 0, relaxed[1], zero)

    state = jnp.concatenate([left, defect, right], axis=1)
    total = strain
    for k in range(1, nt):
        since = (k - 1) % ahead
        if since == 0 and 1 < k < nt - 1:
            tile = state
            state = jnp.concatenate(
                [
                    shifted(tile[:, TILE - ahead:], 1, 1, [k - 1]),
                    shifted(tile, 1, 0, [k - 1]),
                    shifted(tile[:, :ahead], 1, -1, [k - 1]),
                ],
                axis=1,
            )
        else:
            state = shifted(state, 1, 0, [k - 1])
        halo = ahead - since
        got = shifted(total, 1, 0, [k - 1])
        held_p = held_p + got
        if k == nt - 1:
            held = held + state
            break
        out, grown, held = call(
            functools.partial(coarse_kernel, halo),
            [(2, TILE + 2 * halo - 2, *LAYER), (TILE, *LAYER), (2, TILE, *LAYER)],
            [],
            7,
            smem_first=False,
            input_output_aliases={6: 2},
        )(state, tabs, left, defect, right, strain, held)
        total = got + grown
        state = out
    corrected = jnp.stack([held[0], held_p, held[1]])
    return corrected[None], relaxed[None]


def solution(mesh):
    placed = (
        P(None, "space", None, None),
        P("tm", None, "space", None, None),
        P("space", None, None),
    )
    return jax.shard_map(
        functools.partial(on_device, mesh.shape["tm"], mesh.shape["space"]),
        mesh=mesh,
        in_specs=placed,
        out_specs=(P("tm", None, "space", None, None), P("tm", None, "space", None, None)),
        check_vma=False,
    )
```

```python
import functools
import math

import jax
import jax.numpy as jnp
from jax import lax
from jax.experimental import pallas as pl
from jax.experimental.pallas import tpu as pltpu
from jax.sharding import PartitionSpec as P

RATIO = 8
KAPPA = (0.05, 0.08, 0.12, 0.15)
PORE_DIFF = (0.1, 0.04, 0.15, 0.07)
ENERGY = (0.5, 1.0, 1.5, 2.0)
FLUIDITY = (0.2, 0.35, 0.15, 0.3)
STRENGTH = (1.0, 0.6, 1.4, 0.8)
FRICTION_WARMING = 0.3
DRAINAGE = 0.5
DILATANCY = 0.4
TIME_STEP = 0.02
LOG2E = math.log2(math.e)
LN2 = math.log(2.0)

TILE = 8
EXT = 3 * TILE

BLOCKS = ((1, range(2, 3)), (3, range(3, 8)), (9, range(8, 13)), (15, range(13, 16)))
PHASE_END = {k: 7 if k < 8 else 15 for k in range(1, 16)}
ROUNDS = (
    ((15, 13, 13), (9, 10, 10), (3, 4, 4), (1, 2, 2)),
    ((15, 14, 14), (9, 11, 11), (3, 5, 5)),
    ((9, 12, 12), (3, 6, 6)),
    ((9, 8, 8), (3, 7, 7)),
)
KEPT = ((1, 1), (3, 3), (9, 9), (15, 15))
AROUND = 7
VMEM = functools.partial(pl.BlockSpec, memory_space=pltpu.VMEM)
SMEM = functools.partial(pl.BlockSpec, memory_space=pltpu.SMEM)
F32 = jnp.float32


def load_rows(ref, *at):
    return [ref[(*at, pl.ds(r, 8, stride=4), slice(None))] for r in range(4)]


def store_rows(ref, rows, *at):
    for r in range(4):
        ref[(*at, pl.ds(r, 8, stride=4), slice(None))] = rows[r]


def load4(ref, *at):
    *lead, layer = at
    return [ref[(*lead, layer * 4 + r)] for r in range(4)]


def store4(ref, rows, *at):
    *lead, layer = at
    for r in range(4):
        ref[(*lead, layer * 4 + r)] = rows[r]


def loop(low, high, body):
    for start in range(low, high, TILE):
        for layer in range(start, min(start + TILE, high)):
            body(layer, 0)


def edges():
    lane = lax.broadcasted_iota(jnp.int32, (8, 128), 1)
    sub = lax.broadcasted_iota(jnp.int32, (8, 128), 0)
    return lane == 0, lane == 127, sub == 0, sub == 7


def curvature(below, here, above, ends):
    lane0, lane127, sub0, sub7 = ends
    s = [a + b + c for a, b, c in zip(below, here, above)]
    first, second = s[0] + s[1], s[2] + s[3]
    before = jnp.where(sub0, 0.0, pltpu.roll(s[3], 1, 0))
    after = jnp.where(sub7, 0.0, pltpu.roll(s[0], 7, 0))
    columns = [before + first, first + s[2], s[1] + second, second + after]
    out = []
    for c, v in zip(columns, here):
        left = jnp.where(lane0, 0.0, pltpu.roll(c, 1, 1))
        right = jnp.where(lane127, 0.0, pltpu.roll(c, 127, 1))
        out.append((c + left + right) - 27.0 * v)
    return out


def increments(load, tabs, at, ends):
    here_t, here_w = load(0, 0), load(1, 0)
    curve_t = curvature(load(0, -1), here_t, load(0, 1), ends)
    curve_w = curvature(load(1, -1), here_w, load(1, 1), ends)
    hk, hc, c0, c1, s = (load4(tabs, i, at) for i in range(5))
    inc_t, inc_p, inc_w = [], [], []
    for r in range(4):
        warm = 1.0 / (1.5 + jnp.tanh(here_t[r]))
        x = s[r] - 0.5 * here_w[r]
        soft = jnp.maximum(x, 0.0) + LN2 * jnp.log2(1.0 + jnp.exp2(-LOG2E * jnp.abs(x)))
        flow = jnp.exp2(c0[r] - c1[r] * warm) * soft
        inc_t.append(hk[r] * curve_t[r] + FRICTION_WARMING * flow)
        inc_p.append(flow)
        inc_w.append(hc[r] * curve_w[r] - (DRAINAGE * TIME_STEP) * here_w[r] - DILATANCY * flow)
    return here_t, here_w, inc_t, inc_p, inc_w


def plus(a, b):
    return [x + y for x, y in zip(a, b)]


def make_tables(flag, soils, tabs):
    for part, load in enumerate(soils):
        def one(i, _):
            kinds = load(i)
            out = [[] for _ in range(5)]
            for kind in kinds:
                def pick(table):
                    got = jnp.full((8, 128), table[0], F32)
                    for entry in range(1, 4):
                        got = jnp.where(kind == float(entry), F32(table[entry]), got)
                    return got
                rows = [
                    pick([TIME_STEP * v for v in KAPPA]),
                    pick([TIME_STEP * v for v in PORE_DIFF]),
                    pick([LOG2E * e + math.log2(TIME_STEP * f) for e, f in zip(ENERGY, FLUIDITY)]),
                    pick([LOG2E * e for e in ENERGY]),
                    pick(STRENGTH),
                ]
                if part != 1:
                    inside = flag[0 if part == 0 else 1]
                    rows[0], rows[1], rows[3] = rows[0] * inside, rows[1] * inside, rows[3] * inside
                    rows[2] = rows[2] - 1000.0 * (1.0 - inside)
                for o, v in zip(out, rows):
                    o.append(v)
            for k in range(5):
                store4(tabs, out[k], k, part * TILE + i)
            return 0
        lax.fori_loop(0, TILE, one, 0)


def fine_steps(bufs, tabs, ps, finish, ends, first_extra=None):
    for t in range(RATIO):
        src, dst = bufs[t % 2], bufs[(t + 1) % 2]

        def one(l, _, t=t, src=src, dst=dst, tile=False):
            load = lambda f, d: load4(src, f, l + d)
            here_t, here_w, inc_t, inc_p, inc_w = increments(load, tabs, l, ends)
            new_t, new_w = plus(here_t, inc_t), plus(here_w, inc_w)
            if tile:
                i = l - TILE
                if t == 0:
                    store4(ps, inc_p, i)
                    if first_extra is not None:
                        first_extra(i, here_t, here_w, inc_t, inc_p, inc_w)
                else:
                    store4(ps, plus(load4(ps, i), inc_p), i)
            if t == RATIO - 1:
                finish(l - TILE, new_t, new_w)
            else:
                store4(dst, new_t, 0, l)
                store4(dst, new_w, 1, l)
            return 0

        if t < RATIO - 1:
            loop(1 + t, TILE, one)
        loop(TILE, 2 * TILE, functools.partial(one, tile=True))
        if t < RATIO - 1:
            loop(2 * TILE, EXT - 1 - t, one)


def gather_ext(buf, left, centre, right, fields):
    def one(i, _):
        for f, (a, b, c) in enumerate(fields):
            store4(buf, load_rows(left, a, i), f, i)
            store4(buf, load_rows(centre, b, i), f, TILE + i)
            store4(buf, load_rows(right, c, i), f, 2 * TILE + i)
        return 0
    lax.fori_loop(0, TILE, one, 0)


def relax_kernel(flag, centre, pressure, left, right, soil, out, tabs, a, b, ps):
    ends = edges()
    make_tables(
        flag,
        (
            lambda i: load_rows(left, 2, i),
            lambda i: [k.astype(F32) for k in load_rows(soil, i)],
            lambda i: load_rows(right, 2, i),
        ),
        tabs,
    )
    gather_ext(a, left, centre, right, ((0, 0, 0), (1, 1, 1)))

    def finish(i, theta, w):
        store_rows(out, theta, 0, i)
        store_rows(out, w, 2, i)

    fine_steps((a, b), tabs, ps, finish, ends)

    def strain(i, _):
        store_rows(out, plus(load_rows(pressure, i), load4(ps, i)), 1, i)
        return 0
    lax.fori_loop(0, TILE, strain, 0)


def defect_kernel(flag, centre, left, right, tabs, out, out_p, a, b, ps, coarse):
    ends = edges()
    gather_ext(a, left, centre, right, ((0, 0, 0), (1, 2, 1)))
    later = 1.0 - flag[2]

    def first_extra(i, here_t, here_w, inc_t, inc_p, inc_w):
        store4(coarse, [later * (v + RATIO * d) for v, d in zip(here_t, inc_t)], 0, i)
        store4(coarse, [(later * RATIO) * d for d in inc_p], 1, i)
        store4(coarse, [later * (v + RATIO * d) for v, d in zip(here_w, inc_w)], 2, i)

    def finish(i, theta, w):
        store_rows(out, [v - g for v, g in zip(theta, load4(coarse, 0, i))], 0, i)
        store_rows(out, [v - g for v, g in zip(w, load4(coarse, 2, i))], 1, i)

    fine_steps((a, b), tabs, ps, finish, ends, first_extra)

    def strain(i, _):
        rows = zip(load_rows(centre, 1, i), load4(ps, i), load4(coarse, 1, i))
        store_rows(out_p, [flag[2] * p + (s - g) for p, s, g in rows], i)
        return 0
    lax.fori_loop(0, TILE, strain, 0)


def coarse_kernel(halo, state, tabs, defect, out):
    ends = edges()
    new = halo - 1
    wide, narrow = TILE + 2 * halo, TILE + 2 * new

    def one(o, _, tile=False):
        i = o + 1
        load = lambda f, d: load_rows(state, f * wide + i + d)
        here_t, here_w, inc_t, inc_p, inc_w = increments(load, tabs, TILE - halo + i, ends)
        if tile:
            j = o - new
            rows = zip(load_rows(state, 2 * wide + j), inc_p, load_rows(defect, 2 * narrow + j))
            store_rows(out, [(p + RATIO * v) + e for p, v, e in rows], 2 * narrow + j)
        for f, here, inc in ((0, here_t, inc_t), (1, here_w, inc_w)):
            rows = zip(here, inc, load_rows(defect, f * narrow + o))
            store_rows(out, [(v + RATIO * x) + e for v, x, e in rows], f * narrow + o)
        return 0

    loop(0, new, one)
    loop(new, new + TILE, functools.partial(one, tile=True))
    loop(new + TILE, narrow, one)


def call(kernel, outs, scratch, n_in, smem_first=True, **kw):
    specs = [VMEM() for _ in range(n_in)]
    if smem_first:
        specs[0] = SMEM()
    return pl.pallas_call(
        kernel,
        out_shape=[jax.ShapeDtypeStruct(s, F32) for s in outs],
        in_specs=specs,
        out_specs=[VMEM() for _ in outs],
        scratch_shapes=[pltpu.VMEM(s, F32) for s in scratch],
        compiler_params=pltpu.CompilerParams(vmem_limit_bytes=24 * 2**20),
        **kw,
    )


LAYER = (32, 128)
REGS = (8, 128)


def on_device(nt, ns, initial_state, guess, soil):
    t, s = lax.axis_index("tm"), lax.axis_index("space")
    flag = jnp.stack([s > 0, s < ns - 1, t == 0]).astype(F32)
    both = ("tm", "space")

    def shifted(x, dt, ds, only=None):
        pairs = []
        for a in range(nt) if only is None else only:
            for b in range(ns):
                if 0 <= b + ds < ns:
                    pairs.append((a * ns + b, (a + dt) % nt * ns + b + ds))
        return lax.ppermute(x, both, pairs)

    mine = jnp.where(t == nt - 1, initial_state, guess[0])
    heat_stress = jnp.stack([mine[0], mine[2]])
    packed = jnp.concatenate([heat_stress, soil.astype(F32)[None]])
    from_left = shifted(packed, 1, 1)
    from_right = shifted(packed, 1, -1)
    centre = shifted(heat_stress, 1, 0)
    pressure = shifted(mine[1], 1, 0)
    relaxed, tabs = call(
        relax_kernel,
        [(3, TILE, *LAYER), (5, EXT * 4, *REGS)],
        [(2, EXT * 4, *REGS), (2, EXT * 4, *REGS), (TILE * 4, *REGS)],
        6,
    )(flag, centre, pressure, from_left, from_right, soil)

    heat_stress = jnp.stack([relaxed[0], relaxed[2]])
    from_left = shifted(heat_stress, 0, 1)
    from_right = shifted(heat_stress, 0, -1)
    defect, strain = call(
        defect_kernel,
        [(2, TILE, *LAYER), (TILE, *LAYER)],
        [(2, EXT * 4, *REGS), (2, EXT * 4, *REGS), (TILE * 4, *REGS), (3, TILE * 4, *REGS)],
        5,
    )(flag, relaxed, from_left, from_right, tabs)

    around = AROUND
    left = shifted(defect[:, TILE - around:], 0, 1)
    right = shifted(defect[:, :around], 0, -1)
    widened = jnp.concatenate([left, defect, right], axis=1)

    def with_halo(h):
        sides = widened[:, around - h:around + TILE + h]
        return jnp.concatenate([sides.reshape(-1, *LAYER), strain])

    def step(halo, state, term):
        (out,) = call(
            functools.partial(coarse_kernel, halo), [(2 * (TILE + 2 * halo - 2) + TILE, *LAYER)], [], 3, smem_first=False
        )(state, tabs, term)
        return out

    def tile_of(state, h):
        layers = TILE + 2 * h
        return jnp.stack([state[h:h + TILE], state[2 * layers:], state[layers + h:layers + h + TILE]])

    state, holder = with_halo(PHASE_END[2] - 1), 0
    results = {}
    for worker, steps in BLOCKS:
        first = steps[0]
        halo = PHASE_END[first] - first + 1
        hop = worker - holder
        if PHASE_END[first] == PHASE_END[first - 1]:
            state = shifted(state, hop, 0, [holder])
        else:
            tile = state[:2 * TILE]
            before = shifted(tile, hop, 1, [holder])
            after = shifted(tile, hop, -1, [holder])
            state = shifted(state, hop, 0, [holder])
            parts = []
            for f in range(2):
                own = slice(f * TILE, (f + 1) * TILE)
                parts += [before[own][TILE - halo:], state[own], after[own][:halo]]
            state = jnp.concatenate([*parts, state[2 * TILE:]])
        if first == 2:
            results[1] = tile_of(state, halo)
        terms = {}
        for k in steps:
            mine = with_halo(PHASE_END[k] - k)
            terms[k] = mine if k - 1 == worker else shifted(mine, worker - k + 1, 0, [k - 1])
        for k in steps:
            state = step(PHASE_END[k] - k + 1, state, terms[k])
            results[k] = tile_of(state, PHASE_END[k] - k)
        holder = worker

    corrected = jnp.where(t == 0, relaxed, 0.0)
    for sends in ROUNDS:
        payload = results[sends[0][1]]
        pairs = []
        for source, k, target in sends:
            payload = jnp.where(t == source, results[k], payload)
            pairs += [(source * ns + b, target * ns + b) for b in range(ns)]
        corrected = corrected + lax.ppermute(payload, both, pairs)
    for device, k in KEPT:
        corrected = jnp.where(t == device, results[k], corrected)
    return corrected[None], relaxed[None]


def solution(mesh):
    placed = (
        P(None, "space", None, None),
        P("tm", None, "space", None, None),
        P("space", None, None),
    )
    return jax.shard_map(
        functools.partial(on_device, mesh.shape["tm"], mesh.shape["space"]),
        mesh=mesh,
        in_specs=placed,
        out_specs=(P("tm", None, "space", None, None), P("tm", None, "space", None, None)),
        check_vma=False,
    )
```

```python
import functools
import math

import jax
import jax.numpy as jnp
from jax import lax
from jax.experimental import pallas as pl
from jax.experimental.pallas import tpu as pltpu
from jax.sharding import PartitionSpec as P

RATIO = 8
KAPPA = (0.05, 0.08, 0.12, 0.15)
PORE_DIFF = (0.1, 0.04, 0.15, 0.07)
ENERGY = (0.5, 1.0, 1.5, 2.0)
FLUIDITY = (0.2, 0.35, 0.15, 0.3)
STRENGTH = (1.0, 0.6, 1.4, 0.8)
FRICTION_WARMING = 0.3
DRAINAGE = 0.5
DILATANCY = 0.4
TIME_STEP = 0.02
LOG2E = math.log2(math.e)
LN2 = math.log(2.0)

TILE = 8
EXT = 3 * TILE

BLOCKS = ((1, range(2, 3)), (3, range(3, 8)), (9, range(8, 13)), (15, range(13, 16)))
PHASE_END = {k: 7 if k < 8 else 15 for k in range(1, 16)}
GATHERS = (
    (6, ((0, 1), (8, 9))),
    (7, ((2, 3), (7, 9), (14, 15))),
    (3, ((4, 3), (11, 9), (12, 15))),
    (1, ((5, 3), (13, 15))),
    (0, ((6, 3),)),
)
GATHER_WITH_STATE = (5, ((1, 3), (10, 9)))
ROUNDS = (
    ((15, 13, 13), (9, 10, 10), (3, 4, 4), (1, 2, 2)),
    ((15, 14, 14), (9, 11, 11), (3, 5, 5)),
    ((9, 12, 12), (3, 6, 6)),
    ((9, 8, 8), (3, 7, 7)),
)
KEPT = ((1, 1), (3, 3), (9, 9), (15, 15))
AROUND = 7
VMEM = functools.partial(pl.BlockSpec, memory_space=pltpu.VMEM)
SMEM = functools.partial(pl.BlockSpec, memory_space=pltpu.SMEM)
F32 = jnp.float32


def load_rows(ref, *at):
    return [ref[(*at, pl.ds(r, 8, stride=4), slice(None))] for r in range(4)]


def store_rows(ref, rows, *at):
    for r in range(4):
        ref[(*at, pl.ds(r, 8, stride=4), slice(None))] = rows[r]


def load4(ref, *at):
    *lead, layer = at
    return [ref[(*lead, layer * 4 + r)] for r in range(4)]


def store4(ref, rows, *at):
    *lead, layer = at
    for r in range(4):
        ref[(*lead, layer * 4 + r)] = rows[r]


def loop(low, high, body):
    for start in range(low, high, TILE):
        for layer in range(start, min(start + TILE, high)):
            body(layer, 0)


def edges():
    lane = lax.broadcasted_iota(jnp.int32, (8, 128), 1)
    sub = lax.broadcasted_iota(jnp.int32, (8, 128), 0)
    return lane == 0, lane == 127, sub == 0, sub == 7


def curvature(below, here, above, ends):
    lane0, lane127, sub0, sub7 = ends
    s = [a + b + c for a, b, c in zip(below, here, above)]
    first, second = s[0] + s[1], s[2] + s[3]
    before = jnp.where(sub0, 0.0, pltpu.roll(s[3], 1, 0))
    after = jnp.where(sub7, 0.0, pltpu.roll(s[0], 7, 0))
    columns = [before + first, first + s[2], s[1] + second, second + after]
    out = []
    for c, v in zip(columns, here):
        left = jnp.where(lane0, 0.0, pltpu.roll(c, 1, 1))
        right = jnp.where(lane127, 0.0, pltpu.roll(c, 127, 1))
        out.append((c + left + right) - 27.0 * v)
    return out


def increments(load, tabs, at, ends):
    here_t, here_w = load(0, 0), load(1, 0)
    curve_t = curvature(load(0, -1), here_t, load(0, 1), ends)
    curve_w = curvature(load(1, -1), here_w, load(1, 1), ends)
    hk, hc, c0, c1, s = (load4(tabs, i, at) for i in range(5))
    inc_t, inc_p, inc_w = [], [], []
    for r in range(4):
        warm = 1.0 / (1.5 + jnp.tanh(here_t[r]))
        x = s[r] - 0.5 * here_w[r]
        soft = jnp.maximum(x, 0.0) + LN2 * jnp.log2(1.0 + jnp.exp2(-LOG2E * jnp.abs(x)))
        flow = jnp.exp2(c0[r] - c1[r] * warm) * soft
        inc_t.append(hk[r] * curve_t[r] + FRICTION_WARMING * flow)
        inc_p.append(flow)
        inc_w.append(hc[r] * curve_w[r] - (DRAINAGE * TIME_STEP) * here_w[r] - DILATANCY * flow)
    return here_t, here_w, inc_t, inc_p, inc_w


def plus(a, b):
    return [x + y for x, y in zip(a, b)]


def make_tables(flag, soils, tabs):
    for part, load in enumerate(soils):
        def one(i, _):
            kinds = load(i)
            out = [[] for _ in range(5)]
            for kind in kinds:
                def pick(table):
                    got = jnp.full((8, 128), table[0], F32)
                    for entry in range(1, 4):
                        got = jnp.where(kind == float(entry), F32(table[entry]), got)
                    return got
                rows = [
                    pick([TIME_STEP * v for v in KAPPA]),
                    pick([TIME_STEP * v for v in PORE_DIFF]),
                    pick([LOG2E * e + math.log2(TIME_STEP * f) for e, f in zip(ENERGY, FLUIDITY)]),
                    pick([LOG2E * e for e in ENERGY]),
                    pick(STRENGTH),
                ]
                if part != 1:
                    inside = flag[0 if part == 0 else 1]
                    rows[0], rows[1], rows[3] = rows[0] * inside, rows[1] * inside, rows[3] * inside
                    rows[2] = rows[2] - 1000.0 * (1.0 - inside)
                for o, v in zip(out, rows):
                    o.append(v)
            for k in range(5):
                store4(tabs, out[k], k, part * TILE + i)
            return 0
        loop(0, TILE, one)


def fine_steps(bufs, tabs, strain, finish, ends, first_extra=None):
    load_strain, store_strain = strain
    for t in range(RATIO):
        src, dst = bufs[t % 2], bufs[(t + 1) % 2]

        def one(l, _, t=t, src=src, dst=dst, tile=False):
            load = lambda f, d: load4(src, f, l + d)
            here_t, here_w, inc_t, inc_p, inc_w = increments(load, tabs, l, ends)
            new_t, new_w = plus(here_t, inc_t), plus(here_w, inc_w)
            if tile:
                i = l - TILE
                if t == 0:
                    if first_extra is not None:
                        inc_p = first_extra(i, here_t, here_w, inc_t, inc_p, inc_w)
                    store_strain(inc_p, i)
                else:
                    store_strain(plus(load_strain(i), inc_p), i)
            if t == RATIO - 1:
                finish(l - TILE, new_t, new_w)
            else:
                store4(dst, new_t, 0, l)
                store4(dst, new_w, 1, l)
            return 0

        if t < RATIO - 1:
            loop(1 + t, TILE, one)
        loop(TILE, 2 * TILE, functools.partial(one, tile=True))
        if t < RATIO - 1:
            loop(2 * TILE, EXT - 1 - t, one)


def gather_ext(buf, left, centre, right, fields):
    def one(i, _):
        for f, (a, b, c) in enumerate(fields):
            store4(buf, load_rows(left, a, i), f, i)
            store4(buf, load_rows(centre, b, i), f, TILE + i)
            store4(buf, load_rows(right, c, i), f, 2 * TILE + i)
        return 0
    lax.fori_loop(0, TILE, one, 0)


def relax_kernel(flag, centre, left, right, soil, out, ps, tabs, a, b):
    ends = edges()
    make_tables(
        flag,
        (
            lambda i: load_rows(left, 2, i),
            lambda i: [k.astype(F32) for k in load_rows(soil, i)],
            lambda i: load_rows(right, 2, i),
        ),
        tabs,
    )
    gather_ext(a, left, centre, right, ((0, 0, 0), (1, 1, 1)))

    def finish(i, theta, w):
        store_rows(out, theta, 0, i)
        store_rows(out, w, 1, i)

    strain = (lambda i: load4(ps, i), lambda rows, i: store4(ps, rows, i))
    fine_steps((a, b), tabs, strain, finish, ends)


def defect_kernel(flag, centre, left, right, tabs, start_p, first_ps, out, ps, a, b, coarse):
    ends = edges()
    gather_ext(a, left, centre, right, ((0, 0, 0), (1, 1, 1)))
    later = 1.0 - flag[2]

    def first_extra(i, here_t, here_w, inc_t, inc_p, inc_w):
        store4(coarse, [later * (v + RATIO * d) for v, d in zip(here_t, inc_t)], 0, i)
        store4(coarse, [later * (v + RATIO * d) for v, d in zip(here_w, inc_w)], 1, i)
        rows = zip(inc_p, load_rows(start_p, 1, i), load4(first_ps, i))
        return [(1.0 - RATIO * later) * d + flag[2] * (p + q) for d, p, q in rows]

    def finish(i, theta, w):
        store_rows(out, [v - g for v, g in zip(theta, load4(coarse, 0, i))], 0, i)
        store_rows(out, [v - g for v, g in zip(w, load4(coarse, 1, i))], 1, i)

    strain = (lambda i: load_rows(ps, i), lambda rows, i: store_rows(ps, rows, i))
    fine_steps((a, b), tabs, strain, finish, ends, first_extra)


def pack_kernel(halos, left, centre, right, strain, *outs):
    for h, out in zip(halos, outs):
        wide = TILE + 2 * h
        for f in range(2):
            if h:
                out[f * wide:f * wide + h] = left[f, AROUND - h:]
                out[f * wide + h + TILE:(f + 1) * wide] = right[f, :h]
            out[f * wide + h:f * wide + h + TILE] = centre[f]
        out[2 * wide:] = strain[...]


def copy_kernel(*refs):
    n = len(refs) // 2
    for source, target in zip(refs[:n], refs[n + 1:]):
        target[...] = source[...]


def strain_kernel(start_p, ps, out):
    for i in range(TILE):
        store_rows(out, plus(load_rows(start_p, i), load4(ps, i)), i)


def coarse_kernel(halo, sent, state, tabs, defect, out):
    ends = edges()
    new = halo - 1
    wide, narrow, other = TILE + 2 * halo, TILE + 2 * new, TILE + 2 * sent

    def one(o, _, tile=False):
        i = o + 1
        load = lambda f, d: load_rows(state, f * wide + i + d)
        here_t, here_w, inc_t, inc_p, inc_w = increments(load, tabs, TILE - halo + i, ends)
        if tile:
            j = o - new
            rows = zip(load_rows(state, 2 * wide + j), inc_p, load_rows(defect, 2 * other + j))
            store_rows(out, [(p + RATIO * v) + e for p, v, e in rows], 2 * narrow + j)
        for f, here, inc in ((0, here_t, inc_t), (1, here_w, inc_w)):
            rows = zip(here, inc, load_rows(defect, f * other + sent - new + o))
            store_rows(out, [(v + RATIO * x) + e for v, x, e in rows], f * narrow + o)
        return 0

    loop(0, new, one)
    loop(new, new + TILE, functools.partial(one, tile=True))
    loop(new + TILE, narrow, one)


def call(kernel, outs, scratch, specs):
    return pl.pallas_call(
        kernel,
        out_shape=[jax.ShapeDtypeStruct(s, F32) for s in outs],
        in_specs=specs,
        out_specs=[VMEM() for _ in outs],
        scratch_shapes=[pltpu.VMEM(s, F32) for s in scratch],
        compiler_params=pltpu.CompilerParams(vmem_limit_bytes=12 * 2**20),
    )


def after(arrays, wait):
    specs = [VMEM() for _ in arrays] + [pl.BlockSpec(memory_space=pl.ANY)]
    return call(copy_kernel, [a.shape for a in arrays], [], specs)(*arrays, wait)


LAYER = (32, 128)
REGS = (8, 128)


def on_device(nt, ns, initial_state, guess, soil):
    t, s = lax.axis_index("tm"), lax.axis_index("space")
    flag = jnp.stack([s > 0, s < ns - 1, t == 0]).astype(F32)
    both = ("tm", "space")

    def shifted(x, dt, ds, only=None):
        pairs = []
        for a in range(nt) if only is None else only:
            for b in range(ns):
                if 0 <= b + ds < ns:
                    pairs.append((a * ns + b, (a + dt) % nt * ns + b + ds))
        return lax.ppermute(x, both, pairs)

    mine = jnp.where(t == nt - 1, initial_state, guess[0])
    heat_stress = jnp.stack([mine[0], mine[2]])
    packed = jnp.concatenate([heat_stress, soil.astype(F32)[None]])
    from_left = shifted(packed, 1, 1)
    from_right = shifted(packed, 1, -1)
    centre = shifted(heat_stress, 1, 0)
    kept, grown, tabs = call(
        relax_kernel,
        [(2, TILE, *LAYER), (TILE * 4, *REGS), (5, EXT * 4, *REGS)],
        [(2, EXT * 4, *REGS), (2, EXT * 4, *REGS)],
        [SMEM(), *[VMEM() for _ in range(4)]],
    )(flag, centre, from_left, from_right, soil)

    from_left = shifted(kept, 0, 1)
    from_right = shifted(kept, 0, -1)
    defect, strain = call(
        defect_kernel,
        [(2, TILE, *LAYER), (TILE, *LAYER)],
        [(2, EXT * 4, *REGS), (2, EXT * 4, *REGS), (2, TILE * 4, *REGS)],
        [SMEM(), *[VMEM() for _ in range(6)]],
    )(flag, kept, from_left, from_right, tabs, initial_state, grown)

    around = AROUND
    left = shifted(defect[:, TILE - around:], 0, 1)
    right = shifted(defect[:, :around], 0, -1)
    halos = [h for h, _ in GATHERS] + [GATHER_WITH_STATE[0]]
    packs = call(
        functools.partial(pack_kernel, halos),
        [(2 * (TILE + 2 * h) + TILE, *LAYER) for h in halos],
        [],
        [VMEM() for _ in range(4)],
    )(left, defect, right, strain)
    with_halo = dict(zip(halos, packs)).get

    def tile_of(state, h):
        layers = TILE + 2 * h
        return jnp.stack([state[h:h + TILE], state[2 * layers:], state[layers + h:layers + h + TILE]])

    terms = {}

    def gather(payload, h, sends):
        got = lax.ppermute(payload, both, [(a * ns + b, c * ns + b) for a, c in sends for b in range(ns)])
        for a, _ in sends:
            terms[a + 1] = (h, got)
        return got

    def step(k, state):
        halo = PHASE_END[k] - k + 1
        sent, term = terms.get(k) or (halo - 1, with_halo(halo - 1))
        (out,) = call(
            functools.partial(coarse_kernel, halo, sent),
            [(2 * (TILE + 2 * halo - 2) + TILE, *LAYER)],
            [],
            [VMEM() for _ in range(3)],
        )(state, tabs, term)
        return out

    state = [gather(with_halo(h), h, sends) for h, sends in GATHERS][0]
    del terms[1]
    results = {1: tile_of(state, GATHERS[0][0])}
    holder = None
    for worker, steps in BLOCKS:
        first = steps[0]
        halo = PHASE_END[first] - first + 1
        if holder is None:
            pass
        elif holder == BLOCKS[0][0]:
            h, sends = GATHER_WITH_STATE
            state = gather(jnp.where(t == holder, state, with_halo(h)), h, sends)
            del terms[holder + 1]
        elif PHASE_END[first] == PHASE_END[first - 1]:
            state = shifted(state, worker - holder, 0, [holder])
        else:
            hop = worker - holder
            tile = state[:2 * TILE]
            before = shifted(tile, hop, 1, [holder])
            following = shifted(tile, hop, -1, [holder])
            state = shifted(state, hop, 0, [holder])
            parts = []
            for f in range(2):
                own = slice(f * TILE, (f + 1) * TILE)
                parts += [before[own][TILE - halo:], state[own], following[own][:halo]]
            state = jnp.concatenate([*parts, state[2 * TILE:]])
        for k in steps:
            state = step(k, state)
            results[k] = tile_of(state, PHASE_END[k] - k)
        holder = worker

    (start_p,) = after([mine[1]], results[8])
    (relaxed_p,) = call(strain_kernel, [(TILE, *LAYER)], [], [VMEM(), VMEM()])(shifted(start_p, 1, 0), grown)
    relaxed = jnp.stack([kept[0], relaxed_p, kept[1]])
    corrected = jnp.where(t == 0, relaxed, 0.0)
    for sends in ROUNDS:
        payload = results[sends[0][1]]
        pairs = []
        for source, k, target in sends:
            payload = jnp.where(t == source, results[k], payload)
            pairs += [(source * ns + b, target * ns + b) for b in range(ns)]
        corrected = corrected + lax.ppermute(payload, both, pairs)
    for device, k in KEPT:
        corrected = jnp.where(t == device, results[k], corrected)
    return corrected[None], relaxed[None]


def solution(mesh):
    placed = (
        P(None, "space", None, None),
        P("tm", None, "space", None, None),
        P("space", None, None),
    )
    return jax.shard_map(
        functools.partial(on_device, mesh.shape["tm"], mesh.shape["space"]),
        mesh=mesh,
        in_specs=placed,
        out_specs=(P("tm", None, "space", None, None), P("tm", None, "space", None, None)),
        check_vma=False,
    )
```

```python
import functools
import math

import jax
import jax.numpy as jnp
from jax import lax
from jax.experimental import pallas as pl
from jax.experimental.pallas import tpu as pltpu
from jax.sharding import PartitionSpec as P

RATIO = 8
KAPPA = (0.05, 0.08, 0.12, 0.15)
PORE_DIFF = (0.1, 0.04, 0.15, 0.07)
ENERGY = (0.5, 1.0, 1.5, 2.0)
FLUIDITY = (0.2, 0.35, 0.15, 0.3)
STRENGTH = (1.0, 0.6, 1.4, 0.8)
FRICTION_WARMING = 0.3
DRAINAGE = 0.5
DILATANCY = 0.4
TIME_STEP = 0.02
LOG2E = math.log2(math.e)
LN2 = math.log(2.0)

TILE = 8
EXT = 3 * TILE

BLOCKS = ((3, range(2, 8)), (9, range(8, 13)), (15, range(13, 16)))
PHASE_END = {k: 7 if k < 8 else 15 for k in range(1, 16)}
GATHERS = (
    (6, ((0, 3), (8, 9))),
    (5, ((1, 3), (10, 9))),
    (3, ((4, 3), (11, 9), (12, 15))),
    (7, ((2, 3), (7, 9), (14, 15))),
    (1, ((5, 3), (13, 15))),
    (0, ((6, 3),)),
)
ROUNDS = (
    ((9, 12, 12), (3, 7, 7)),
    ((9, 11, 11), (3, 6, 6)),
    ((9, 8, 8), (3, 2, 2)),
    ((15, 13, 13), (9, 10, 10), (3, 4, 4), (0, 1, 1)),
    ((15, 14, 14), (3, 5, 5)),
)
KEPT = ((3, 3), (9, 9), (15, 15))
AROUND = 7
VMEM = functools.partial(pl.BlockSpec, memory_space=pltpu.VMEM)
SMEM = functools.partial(pl.BlockSpec, memory_space=pltpu.SMEM)
F32 = jnp.float32


def load_rows(ref, *at):
    return [ref[(*at, pl.ds(r, 8, stride=4), slice(None))] for r in range(4)]


def store_rows(ref, rows, *at):
    for r in range(4):
        ref[(*at, pl.ds(r, 8, stride=4), slice(None))] = rows[r]


def load4(ref, *at):
    *lead, layer = at
    return [ref[(*lead, layer * 4 + r)] for r in range(4)]


def store4(ref, rows, *at):
    *lead, layer = at
    for r in range(4):
        ref[(*lead, layer * 4 + r)] = rows[r]


def loop(low, high, body):
    for start in range(low, high, TILE):
        for layer in range(start, min(start + TILE, high)):
            body(layer, 0)


def edges():
    lane = lax.broadcasted_iota(jnp.int32, (8, 128), 1)
    sub = lax.broadcasted_iota(jnp.int32, (8, 128), 0)
    return lane == 0, lane == 127, sub == 0, sub == 7


def curvature(below, here, above, ends):
    lane0, lane127, sub0, sub7 = ends
    s = [a + b + c for a, b, c in zip(below, here, above)]
    first, second = s[0] + s[1], s[2] + s[3]
    before = jnp.where(sub0, 0.0, pltpu.roll(s[3], 1, 0))
    after = jnp.where(sub7, 0.0, pltpu.roll(s[0], 7, 0))
    columns = [before + first, first + s[2], s[1] + second, second + after]
    out = []
    for c, v in zip(columns, here):
        left = jnp.where(lane0, 0.0, pltpu.roll(c, 1, 1))
        right = jnp.where(lane127, 0.0, pltpu.roll(c, 127, 1))
        out.append((c + left + right) - 27.0 * v)
    return out


def increments(load, tabs, at, ends):
    here_t, here_w = load(0, 0), load(1, 0)
    curve_t = curvature(load(0, -1), here_t, load(0, 1), ends)
    curve_w = curvature(load(1, -1), here_w, load(1, 1), ends)
    hk, hc, c0, c1, s = (load4(tabs, i, at) for i in range(5))
    inc_t, inc_p, inc_w = [], [], []
    for r in range(4):
        warm = 1.0 / (1.5 + jnp.tanh(here_t[r]))
        x = s[r] - 0.5 * here_w[r]
        soft = jnp.maximum(x, 0.0) + LN2 * jnp.log2(1.0 + jnp.exp2(-LOG2E * jnp.abs(x)))
        flow = jnp.exp2(c0[r] - c1[r] * warm) * soft
        inc_t.append(hk[r] * curve_t[r] + FRICTION_WARMING * flow)
        inc_p.append(flow)
        inc_w.append(hc[r] * curve_w[r] - (DRAINAGE * TIME_STEP) * here_w[r] - DILATANCY * flow)
    return here_t, here_w, inc_t, inc_p, inc_w


def plus(a, b):
    return [x + y for x, y in zip(a, b)]


def make_tables(place, last, soils, tabs):
    for part, load in enumerate(soils):
        def one(i, _):
            kinds = load(i)
            out = [[] for _ in range(5)]
            for kind in kinds:
                def pick(table):
                    got = jnp.full((8, 128), table[0], F32)
                    for entry in range(1, 4):
                        got = jnp.where(kind == float(entry), F32(table[entry]), got)
                    return got
                rows = [
                    pick([TIME_STEP * v for v in KAPPA]),
                    pick([TIME_STEP * v for v in PORE_DIFF]),
                    pick([LOG2E * e + math.log2(TIME_STEP * f) for e, f in zip(ENERGY, FLUIDITY)]),
                    pick([LOG2E * e for e in ENERGY]),
                    pick(STRENGTH),
                ]
                if part != 1:
                    inside = (place[1] > 0) if part == 0 else (place[1] < last)
                    rows = [jnp.where(inside, v, other) for v, other in zip(rows, (0.0, 0.0, -1000.0, 0.0, 0.0))]
                for o, v in zip(out, rows):
                    o.append(v)
            for k in range(5):
                store4(tabs, out[k], k, part * TILE + i)
            return 0
        loop(0, TILE, one)


def fine_steps(bufs, tabs, strain, finish, ends, first_extra=None):
    load_strain, store_strain = strain
    for t in range(RATIO):
        src, dst = bufs[t % 2], bufs[(t + 1) % 2]

        def one(l, _, t=t, src=src, dst=dst, tile=False):
            load = lambda f, d: load4(src, f, l + d)
            here_t, here_w, inc_t, inc_p, inc_w = increments(load, tabs, l, ends)
            new_t, new_w = plus(here_t, inc_t), plus(here_w, inc_w)
            if tile:
                i = l - TILE
                if t == 0:
                    if first_extra is not None:
                        inc_p = first_extra(i, here_t, here_w, inc_t, inc_p, inc_w)
                    store_strain(inc_p, i)
                else:
                    store_strain(plus(load_strain(i), inc_p), i)
            if t == RATIO - 1:
                finish(l - TILE, new_t, new_w)
            else:
                store4(dst, new_t, 0, l)
                store4(dst, new_w, 1, l)
            return 0

        if t < RATIO - 1:
            loop(1 + t, TILE, one)
        loop(TILE, 2 * TILE, functools.partial(one, tile=True))
        if t < RATIO - 1:
            loop(2 * TILE, EXT - 1 - t, one)


def gather_ext(buf, left, centre, right, fields):
    def one(i, _):
        for f, (a, b, c) in enumerate(fields):
            store4(buf, load_rows(left, a, i), f, i)
            store4(buf, load_rows(centre, b, i), f, TILE + i)
            store4(buf, load_rows(right, c, i), f, 2 * TILE + i)
        return 0
    lax.fori_loop(0, TILE, one, 0)


def relax_kernel(last, place, centre, left, right, soil, out, ps, tabs, a, b):
    ends = edges()
    make_tables(
        place,
        last,
        (
            lambda i: load_rows(left, 2, i),
            lambda i: load_rows(soil, 2, i),
            lambda i: load_rows(right, 2, i),
        ),
        tabs,
    )
    gather_ext(a, left, centre, right, ((0, 0, 0), (1, 1, 1)))

    def finish(i, theta, w):
        store_rows(out, theta, 0, i)
        store_rows(out, w, 1, i)

    strain = (lambda i: load4(ps, i), lambda rows, i: store4(ps, rows, i))
    fine_steps((a, b), tabs, strain, finish, ends)


def defect_kernel(place, centre, left, right, tabs, start_p, first_ps, out, up, down, ps, a, b, coarse):
    ends = edges()
    gather_ext(a, left, centre, right, ((0, 0, 0), (1, 1, 1)))
    first = jnp.where(place[0] == 0, 1.0, 0.0)
    later = 1.0 - first

    def first_extra(i, here_t, here_w, inc_t, inc_p, inc_w):
        store4(coarse, [later * (v + RATIO * d) for v, d in zip(here_t, inc_t)], 0, i)
        store4(coarse, [later * (v + RATIO * d) for v, d in zip(here_w, inc_w)], 1, i)
        rows = zip(inc_p, load_rows(start_p, 1, i), load4(first_ps, i))
        return [(1.0 - RATIO * later) * d + first * (p + q) for d, p, q in rows]

    def finish(i, theta, w):
        for f, rows in enumerate((theta, w)):
            rows = [v - g for v, g in zip(rows, load4(coarse, f, i))]
            store_rows(out, rows, f, i)
            if i >= TILE - AROUND:
                store_rows(up, rows, f, i - (TILE - AROUND))
            if i < AROUND:
                store_rows(down, rows, f, i)

    strain = (lambda i: load_rows(ps, i), lambda rows, i: store_rows(ps, rows, i))
    fine_steps((a, b), tabs, strain, finish, ends, first_extra)


def pack_kernel(halos, left, centre, right, strain, *outs):
    for h, out in zip(halos, outs):
        wide = TILE + 2 * h
        for f in range(2):
            if h:
                out[f * wide:f * wide + h] = left[f, AROUND - h:]
                out[f * wide + h + TILE:(f + 1) * wide] = right[f, :h]
            out[f * wide + h:f * wide + h + TILE] = centre[f]
        out[2 * wide:] = strain[...]


def join_kernel(before, state, after, out):
    for f in range(2):
        for part, (ref, at) in enumerate(((before, f * TILE), (state, f * TILE), (after, f * TILE))):
            out[f * EXT + part * TILE:f * EXT + (part + 1) * TILE] = ref[at:at + TILE]
    out[2 * EXT:] = state[2 * TILE:]


def copy_tile(out, state, h):
    layers = TILE + 2 * h
    out[0] = state[h:h + TILE]
    out[1] = state[2 * layers:]
    out[2] = state[layers + h:layers + h + TILE]


def send_kernel(plan, place, *refs):
    *states, out = refs
    for (sender, h), state in zip(plan, states):
        pl.when(place[0] == sender)(functools.partial(copy_tile, out, state, h))


def corrected_kernel(kept, sent, place, relaxed, *refs):
    *results, out = refs

    @pl.when(place[0] == 0)
    def _():
        out[...] = relaxed[...]

    for (device, h), state in zip(kept, results):
        pl.when(place[0] == device)(functools.partial(copy_tile, out, state, h))
    for devices, got in zip(sent, results[len(kept):]):
        for device in devices:
            @pl.when(place[0] == device)
            def _(got=got):
                out[...] = got[...]


def late_kernel(start_p, wait, out):
    out[...] = start_p[...]


def relaxed_kernel(place, start_p, first_p, kept, ps, *outs):
    is_first = place[0] == 0
    rows = [
        [jnp.where(is_first, a, b) for a, b in zip(load_rows(first_p, 1, i), load_rows(start_p, i))] for i in range(TILE)
    ]
    for out in outs:
        out[0], out[2] = kept[0], kept[1]
        for i in range(TILE):
            store_rows(out, plus(rows[i], load4(ps, i)), 1, i)


def coarse_kernel(halo, sent, waits, state, tabs, defect, *rest):
    out, *tile_out = rest[waits:]
    tile_out = tile_out[0] if tile_out else None
    ends = edges()
    new = halo - 1
    wide, narrow, other = TILE + 2 * halo, TILE + 2 * new, TILE + 2 * sent

    def one(o, _, tile=False):
        i = o + 1
        load = lambda f, d: load_rows(state, f * wide + i + d)
        here_t, here_w, inc_t, inc_p, inc_w = increments(load, tabs, TILE - halo + i, ends)
        if tile:
            j = o - new
            rows = zip(load_rows(state, 2 * wide + j), inc_p, load_rows(defect, 2 * other + j))
            store_rows(out, [(p + RATIO * v) + e for p, v, e in rows], 2 * narrow + j)
        for f, here, inc in ((0, here_t, inc_t), (1, here_w, inc_w)):
            rows = zip(here, inc, load_rows(defect, f * other + sent - new + o))
            rows = [(v + RATIO * x) + e for v, x, e in rows]
            store_rows(out, rows, f * narrow + o)
            if tile_out is not None:
                store_rows(tile_out, rows, f * narrow + o)
        return 0

    loop(0, new, one)
    loop(new, new + TILE, functools.partial(one, tile=True))
    loop(new + TILE, narrow, one)


def call(kernel, outs, scratch, operands, place=None, waits=()):
    specs = [VMEM() for _ in operands] + [pl.BlockSpec(memory_space=pltpu.HBM if x.size > 2 * TILE * 32 * 128 else pl.ANY) for x in waits]
    operands = [*operands, *waits]
    if place is not None:
        operands, specs = [place, *operands], [SMEM(), *specs]
    return pl.pallas_call(
        kernel,
        out_shape=[jax.ShapeDtypeStruct(s, F32) for s in outs],
        in_specs=specs,
        out_specs=[VMEM() for _ in outs],
        scratch_shapes=[pltpu.VMEM(s, F32) if isinstance(s, tuple) else s for s in scratch],
        compiler_params=pltpu.CompilerParams(vmem_limit_bytes=12 * 2**20),
        cost_estimate=pl.CostEstimate(flops=1, bytes_accessed=1, transcendentals=0),
    )(*operands)


LAYER = (32, 128)
REGS = (8, 128)


def on_device(nt, ns, initial_state, guess, soil):
    place = jnp.stack([lax.axis_index("tm"), lax.axis_index("space")]).astype(jnp.int32)
    both = ("tm", "space")
    tile, whole = (2, TILE, *LAYER), (3, TILE, *LAYER)

    def sent(x, moves, ds=0):
        pairs = [(a * ns + b, c * ns + b + ds) for a, c in moves for b in range(ns) if 0 <= b + ds < ns]
        return lax.ppermute(x, both, pairs)

    stay = [(a, a) for a in range(nt)]
    ahead = [(a, (a + 1) % nt) for a in range(nt)]

    mine = jnp.where(lax.axis_index("tm") == nt - 1, initial_state, guess[0])
    mine_p, heat_stress = mine[1], jnp.stack([mine[0], mine[2]])
    packed = jnp.concatenate([heat_stress, soil.astype(F32)[None]])
    from_left = sent(packed, ahead, 1)
    from_right = sent(packed, ahead, -1)
    centre = sent(heat_stress, ahead)
    kept, grown, tabs = call(
        functools.partial(relax_kernel, ns - 1),
        [tile, (TILE * 4, *REGS), (5, EXT * 4, *REGS)],
        [(2, EXT * 4, *REGS), (2, EXT * 4, *REGS)],
        [centre, from_left, from_right, packed],
        place,
    )

    from_left = sent(kept, stay, 1)
    from_right = sent(kept, stay, -1)
    around = (2, AROUND, *LAYER)
    defect, up, down, strain = call(
        defect_kernel,
        [tile, around, around, (TILE, *LAYER)],
        [(2, EXT * 4, *REGS), (2, EXT * 4, *REGS), (2, TILE * 4, *REGS)],
        [kept, from_left, from_right, tabs, initial_state, grown],
        place,
    )
    left, right = sent(up, stay, 1), sent(down, stay, -1)
    halos = [h for h, _ in GATHERS]
    packs = call(
        functools.partial(pack_kernel, halos),
        [(2 * (TILE + 2 * h) + TILE, *LAYER) for h in halos],
        [],
        [left, defect, right, strain],
    )
    with_halo = dict(zip(halos, packs))

    terms = {}
    for h, moves in GATHERS:
        got = sent(with_halo[h], moves)
        for a, _ in moves:
            terms[a + 1] = (h, got)
    results = {1: terms.pop(1)}
    state, holder, late = results[1][1], None, 3
    for worker, steps in BLOCKS:
        first = steps[0]
        halo = PHASE_END[first] - first + 1
        if holder is None:
            pass
        elif PHASE_END[first] == PHASE_END[first - 1]:
            state = sent(state, [(holder, worker)])
        else:
            move = [(holder, worker)]
            parts = sent(edge, move, 1), sent(state, move), sent(edge, move, -1)
            (state,) = call(join_kernel, [(2 * EXT + TILE, *LAYER)], [], parts)
        waits = [held] if late in results and first == PHASE_END[late] + 1 else []
        for k in steps:
            halo = PHASE_END[k] - k + 1
            given, term = terms.get(k) or (halo - 1, with_halo[halo - 1])
            shapes = [(2 * (TILE + 2 * halo - 2) + TILE, *LAYER)]
            if halo == 1 and k < nt - 1:
                shapes.append((2 * TILE, *LAYER))
            state, *edge = call(
                functools.partial(coarse_kernel, halo, given, len(waits)), shapes, [], [state, tabs, term], waits=waits
            )
            edge = edge[0] if edge else None
            results[k] = (halo - 1, state)
            waits = []
            if k == late:
                (late_p,) = call(late_kernel, [(TILE, *LAYER)], [], [mine_p], waits=[state])
                relaxed, held = call(
                    relaxed_kernel, [whole, whole], [], [sent(late_p, ahead[:-1]), initial_state, kept, grown], place
                )
        holder = worker

    results[1] = (0, with_halo[0])
    received = []
    for sends in ROUNDS:
        plan = [(source, results[k][0]) for source, k, _ in sends]
        (payload,) = call(
            functools.partial(send_kernel, plan), [whole], [], [results[k][1] for _, k, _ in sends], place
        )
        received.append(sent(payload, [(source, target) for source, _, target in sends]))
    (corrected,) = call(
        functools.partial(
            corrected_kernel,
            [(device, results[k][0]) for device, k in KEPT],
            [[target for _, _, target in sends] for sends in ROUNDS],
        ),
        [whole],
        [],
        [held, *[results[k][1] for _, k in KEPT], *received],
        place,
    )
    return corrected[None], relaxed[None]


def solution(mesh):
    placed = (
        P(None, "space", None, None),
        P("tm", None, "space", None, None),
        P("space", None, None),
    )
    return jax.shard_map(
        functools.partial(on_device, mesh.shape["tm"], mesh.shape["space"]),
        mesh=mesh,
        in_specs=placed,
        out_specs=(P("tm", None, "space", None, None), P("tm", None, "space", None, None)),
        check_vma=False,
    )
```

```python
import functools
import math

import jax
import jax.numpy as jnp
from jax import lax
from jax.experimental import pallas as pl
from jax.experimental.pallas import tpu as pltpu
from jax.sharding import PartitionSpec as P

RATIO = 8
KAPPA = (0.05, 0.08, 0.12, 0.15)
PORE_DIFF = (0.1, 0.04, 0.15, 0.07)
ENERGY = (0.5, 1.0, 1.5, 2.0)
FLUIDITY = (0.2, 0.35, 0.15, 0.3)
STRENGTH = (1.0, 0.6, 1.4, 0.8)
FRICTION_WARMING = 0.3
DRAINAGE = 0.5
DILATANCY = 0.4
TIME_STEP = 0.02
LOG2E = math.log2(math.e)
LN2 = math.log(2.0)

TILE = 8
EXT = 3 * TILE

BLOCKS = ((3, range(2, 8)), (9, range(8, 13)), (15, range(13, 16)))
PHASE_END = {k: 7 if k < 8 else 15 for k in range(1, 16)}
GATHERS = (
    (6, ((0, 3), (8, 9))),
    (5, ((1, 3), (10, 9))),
    (3, ((4, 3), (11, 9), (12, 15))),
    (7, ((2, 3), (7, 9), (14, 15))),
    (1, ((5, 3), (13, 15))),
    (0, ((6, 3),)),
)
ROUNDS = (
    ((9, 12, 12), (3, 7, 7)),
    ((9, 11, 11), (3, 6, 6)),
    ((9, 8, 8), (3, 2, 2)),
    ((15, 13, 13), (9, 10, 10), (3, 4, 4), (0, 1, 1)),
    ((15, 14, 14), (3, 5, 5)),
)
KEPT = ((3, 3), (9, 9), (15, 15))
AROUND = 7
VMEM = functools.partial(pl.BlockSpec, memory_space=pltpu.VMEM)
SMEM = functools.partial(pl.BlockSpec, memory_space=pltpu.SMEM)
F32 = jnp.float32


def load_rows(ref, *at):
    return [ref[(*at, pl.ds(r, 8, stride=4), slice(None))] for r in range(4)]


def store_rows(ref, rows, *at):
    for r in range(4):
        ref[(*at, pl.ds(r, 8, stride=4), slice(None))] = rows[r]


def load4(ref, *at):
    *lead, layer = at
    return [ref[(*lead, layer * 4 + r)] for r in range(4)]


def store4(ref, rows, *at):
    *lead, layer = at
    for r in range(4):
        ref[(*lead, layer * 4 + r)] = rows[r]


def loop(low, high, body):
    for start in range(low, high, TILE):
        for layer in range(start, min(start + TILE, high)):
            body(layer, 0)


def edges():
    lane = lax.broadcasted_iota(jnp.int32, (8, 128), 1)
    sub = lax.broadcasted_iota(jnp.int32, (8, 128), 0)
    return lane == 0, lane == 127, sub == 0, sub == 7


def curvature(below, here, above, ends):
    lane0, lane127, sub0, sub7 = ends
    s = [a + b + c for a, b, c in zip(below, here, above)]
    first, second = s[0] + s[1], s[2] + s[3]
    before = jnp.where(sub0, 0.0, pltpu.roll(s[3], 1, 0))
    after = jnp.where(sub7, 0.0, pltpu.roll(s[0], 7, 0))
    columns = [before + first, first + s[2], s[1] + second, second + after]
    out = []
    for c, v in zip(columns, here):
        left = jnp.where(lane0, 0.0, pltpu.roll(c, 1, 1))
        right = jnp.where(lane127, 0.0, pltpu.roll(c, 127, 1))
        out.append((c + left + right) - 27.0 * v)
    return out


def increments(load, tabs, at, ends):
    here_t, here_w = load(0, 0), load(1, 0)
    curve_t = curvature(load(0, -1), here_t, load(0, 1), ends)
    curve_w = curvature(load(1, -1), here_w, load(1, 1), ends)
    hk, hc, c0, c1, s = (load4(tabs, i, at) for i in range(5))
    inc_t, inc_p, inc_w = [], [], []
    for r in range(4):
        base = 1.5 + jnp.tanh(here_t[r])
        warm = pl.reciprocal(base, approx=True)
        warm = warm * (2.0 - base * warm)
        warm = warm * (2.0 - base * warm)
        x = s[r] - 0.5 * here_w[r]
        soft = jnp.maximum(x, 0.0) + LN2 * jnp.log2(1.0 + jnp.exp2(-LOG2E * jnp.abs(x)))
        flow = jnp.exp2(c0[r] - c1[r] * warm) * soft
        inc_t.append(hk[r] * curve_t[r] + FRICTION_WARMING * flow)
        inc_p.append(flow)
        inc_w.append(hc[r] * curve_w[r] - (DRAINAGE * TIME_STEP) * here_w[r] - DILATANCY * flow)
    return here_t, here_w, inc_t, inc_p, inc_w


def plus(a, b):
    return [x + y for x, y in zip(a, b)]


def make_tables(place, last, soils, tabs):
    for part, load in enumerate(soils):
        def one(i, _):
            kinds = load(i)
            out = [[] for _ in range(5)]
            for kind in kinds:
                def pick(table):
                    got = jnp.full((8, 128), table[0], F32)
                    for entry in range(1, 4):
                        got = jnp.where(kind == float(entry), F32(table[entry]), got)
                    return got
                rows = [
                    pick([TIME_STEP * v for v in KAPPA]),
                    pick([TIME_STEP * v for v in PORE_DIFF]),
                    pick([LOG2E * e + math.log2(TIME_STEP * f) for e, f in zip(ENERGY, FLUIDITY)]),
                    pick([LOG2E * e for e in ENERGY]),
                    pick(STRENGTH),
                ]
                if part != 1:
                    inside = (place[1] > 0) if part == 0 else (place[1] < last)
                    rows = [jnp.where(inside, v, other) for v, other in zip(rows, (0.0, 0.0, -1000.0, 0.0, 0.0))]
                for o, v in zip(out, rows):
                    o.append(v)
            for k in range(5):
                store4(tabs, out[k], k, part * TILE + i)
            return 0
        loop(0, TILE, one)


def fine_steps(bufs, tabs, strain, finish, ends, first_extra=None):
    load_strain, store_strain = strain
    for t in range(RATIO):
        src, dst = bufs[t % 2], bufs[(t + 1) % 2]

        def one(l, _, t=t, src=src, dst=dst, tile=False):
            load = lambda f, d: load4(src, f, l + d)
            here_t, here_w, inc_t, inc_p, inc_w = increments(load, tabs, l, ends)
            new_t, new_w = plus(here_t, inc_t), plus(here_w, inc_w)
            if tile:
                i = l - TILE
                if t == 0:
                    if first_extra is not None:
                        inc_p = first_extra(i, here_t, here_w, inc_t, inc_p, inc_w)
                    store_strain(inc_p, i)
                else:
                    store_strain(plus(load_strain(i), inc_p), i)
            if t == RATIO - 1:
                finish(l - TILE, new_t, new_w)
            else:
                store4(dst, new_t, 0, l)
                store4(dst, new_w, 1, l)
            return 0

        if t < RATIO - 1:
            loop(1 + t, TILE, one)
        loop(TILE, 2 * TILE, functools.partial(one, tile=True))
        if t < RATIO - 1:
            loop(2 * TILE, EXT - 1 - t, one)


def gather_ext(buf, left, centre, right, fields):
    def one(i, _):
        for f, (a, b, c) in enumerate(fields):
            store4(buf, load_rows(left, a, i), f, i)
            store4(buf, load_rows(centre, b, i), f, TILE + i)
            store4(buf, load_rows(right, c, i), f, 2 * TILE + i)
        return 0
    lax.fori_loop(0, TILE, one, 0)


def relax_kernel(last, place, centre, left, right, soil, out, ps, tabs, a, b):
    ends = edges()
    make_tables(
        place,
        last,
        (
            lambda i: load_rows(left, 2, i),
            lambda i: load_rows(soil, 2, i),
            lambda i: load_rows(right, 2, i),
        ),
        tabs,
    )
    gather_ext(a, left, centre, right, ((0, 0, 0), (1, 1, 1)))

    def finish(i, theta, w):
        store_rows(out, theta, 0, i)
        store_rows(out, w, 1, i)

    strain = (lambda i: load4(ps, i), lambda rows, i: store4(ps, rows, i))
    fine_steps((a, b), tabs, strain, finish, ends)


def defect_kernel(place, centre, left, right, tabs, start_p, first_ps, out, up, down, ps, a, b, coarse):
    ends = edges()
    gather_ext(a, left, centre, right, ((0, 0, 0), (1, 1, 1)))
    first = jnp.where(place[0] == 0, 1.0, 0.0)
    later = 1.0 - first

    def first_extra(i, here_t, here_w, inc_t, inc_p, inc_w):
        store4(coarse, [later * (v + RATIO * d) for v, d in zip(here_t, inc_t)], 0, i)
        store4(coarse, [later * (v + RATIO * d) for v, d in zip(here_w, inc_w)], 1, i)
        rows = zip(inc_p, load_rows(start_p, 1, i), load4(first_ps, i))
        return [(1.0 - RATIO * later) * d + first * (p + q) for d, p, q in rows]

    def finish(i, theta, w):
        for f, rows in enumerate((theta, w)):
            rows = [v - g for v, g in zip(rows, load4(coarse, f, i))]
            store_rows(out, rows, f, i)
            if i >= TILE - AROUND:
                store_rows(up, rows, f, i - (TILE - AROUND))
            if i < AROUND:
                store_rows(down, rows, f, i)

    strain = (lambda i: load_rows(ps, i), lambda rows, i: store_rows(ps, rows, i))
    fine_steps((a, b), tabs, strain, finish, ends, first_extra)


def pack_kernel(halos, left, centre, right, strain, *outs):
    for h, out in zip(halos, outs):
        wide = TILE + 2 * h
        for f in range(2):
            if h:
                out[f * wide:f * wide + h] = left[f, AROUND - h:]
                out[f * wide + h + TILE:(f + 1) * wide] = right[f, :h]
            out[f * wide + h:f * wide + h + TILE] = centre[f]
        out[2 * wide:] = strain[...]


def join_kernel(before, state, after, out):
    for f in range(2):
        for part, (ref, at) in enumerate(((before, f * TILE), (state, f * TILE), (after, f * TILE))):
            out[f * EXT + part * TILE:f * EXT + (part + 1) * TILE] = ref[at:at + TILE]
    out[2 * EXT:] = state[2 * TILE:]


def copy_tile(out, state, h):
    layers = TILE + 2 * h
    out[0] = state[h:h + TILE]
    out[1] = state[2 * layers:]
    out[2] = state[layers + h:layers + h + TILE]


def send_kernel(plan, place, *refs):
    *states, out = refs
    for (sender, h), state in zip(plan, states):
        pl.when(place[0] == sender)(functools.partial(copy_tile, out, state, h))


def corrected_kernel(kept, sent, place, relaxed, *refs):
    *results, out = refs

    @pl.when(place[0] == 0)
    def _():
        out[...] = relaxed[...]

    for (device, h), state in zip(kept, results):
        pl.when(place[0] == device)(functools.partial(copy_tile, out, state, h))
    for devices, got in zip(sent, results[len(kept):]):
        for device in devices:
            @pl.when(place[0] == device)
            def _(got=got):
                out[...] = got[...]


def late_kernel(start_p, wait, out):
    out[...] = start_p[...]


def relaxed_kernel(place, start_p, first_p, kept, ps, *outs):
    is_first = place[0] == 0
    rows = [
        [jnp.where(is_first, a, b) for a, b in zip(load_rows(first_p, 1, i), load_rows(start_p, i))] for i in range(TILE)
    ]
    for out in outs:
        out[0], out[2] = kept[0], kept[1]
        for i in range(TILE):
            store_rows(out, plus(rows[i], load4(ps, i)), 1, i)


def coarse_kernel(halo, sent, waits, state, tabs, defect, *rest):
    out, *tile_out = rest[waits:]
    tile_out = tile_out[0] if tile_out else None
    ends = edges()
    new = halo - 1
    wide, narrow, other = TILE + 2 * halo, TILE + 2 * new, TILE + 2 * sent

    def one(o, _, tile=False):
        i = o + 1
        load = lambda f, d: load_rows(state, f * wide + i + d)
        here_t, here_w, inc_t, inc_p, inc_w = increments(load, tabs, TILE - halo + i, ends)
        if tile:
            j = o - new
            rows = zip(load_rows(state, 2 * wide + j), inc_p, load_rows(defect, 2 * other + j))
            store_rows(out, [(p + RATIO * v) + e for p, v, e in rows], 2 * narrow + j)
        for f, here, inc in ((0, here_t, inc_t), (1, here_w, inc_w)):
            rows = zip(here, inc, load_rows(defect, f * other + sent - new + o))
            rows = [(v + RATIO * x) + e for v, x, e in rows]
            store_rows(out, rows, f * narrow + o)
            if tile_out is not None:
                store_rows(tile_out, rows, f * narrow + o)
        return 0

    loop(0, new, one)
    loop(new, new + TILE, functools.partial(one, tile=True))
    loop(new + TILE, narrow, one)


def call(kernel, outs, scratch, operands, place=None, waits=()):
    specs = [VMEM() for _ in operands] + [pl.BlockSpec(memory_space=pltpu.HBM if x.size > 2 * TILE * 32 * 128 else pl.ANY) for x in waits]
    operands = [*operands, *waits]
    if place is not None:
        operands, specs = [place, *operands], [SMEM(), *specs]
    return pl.pallas_call(
        kernel,
        out_shape=[jax.ShapeDtypeStruct(s, F32) for s in outs],
        in_specs=specs,
        out_specs=[VMEM() for _ in outs],
        scratch_shapes=[pltpu.VMEM(s, F32) if isinstance(s, tuple) else s for s in scratch],
        compiler_params=pltpu.CompilerParams(vmem_limit_bytes=12 * 2**20),
        cost_estimate=pl.CostEstimate(flops=1, bytes_accessed=1, transcendentals=0),
    )(*operands)


LAYER = (32, 128)
REGS = (8, 128)


def on_device(nt, ns, initial_state, guess, soil):
    place = jnp.stack([lax.axis_index("tm"), lax.axis_index("space")]).astype(jnp.int32)
    both = ("tm", "space")
    tile, whole = (2, TILE, *LAYER), (3, TILE, *LAYER)

    def sent(x, moves, ds=0):
        pairs = [(a * ns + b, c * ns + b + ds) for a, c in moves for b in range(ns) if 0 <= b + ds < ns]
        return lax.ppermute(x, both, pairs)

    stay = [(a, a) for a in range(nt)]
    ahead = [(a, (a + 1) % nt) for a in range(nt)]

    mine = jnp.where(lax.axis_index("tm") == nt - 1, initial_state, guess[0])
    mine_p, heat_stress = mine[1], jnp.stack([mine[0], mine[2]])
    packed = jnp.concatenate([heat_stress, soil.astype(F32)[None]])
    from_left = sent(packed, ahead, 1)
    from_right = sent(packed, ahead, -1)
    centre = sent(heat_stress, ahead)
    kept, grown, tabs = call(
        functools.partial(relax_kernel, ns - 1),
        [tile, (TILE * 4, *REGS), (5, EXT * 4, *REGS)],
        [(2, EXT * 4, *REGS), (2, EXT * 4, *REGS)],
        [centre, from_left, from_right, packed],
        place,
    )

    from_left = sent(kept, stay, 1)
    from_right = sent(kept, stay, -1)
    around = (2, AROUND, *LAYER)
    defect, up, down, strain = call(
        defect_kernel,
        [tile, around, around, (TILE, *LAYER)],
        [(2, EXT * 4, *REGS), (2, EXT * 4, *REGS), (2, TILE * 4, *REGS)],
        [kept, from_left, from_right, tabs, initial_state, grown],
        place,
    )
    left, right = sent(up, stay, 1), sent(down, stay, -1)
    halos = [h for h, _ in GATHERS]
    packs = call(
        functools.partial(pack_kernel, halos),
        [(2 * (TILE + 2 * h) + TILE, *LAYER) for h in halos],
        [],
        [left, defect, right, strain],
    )
    with_halo = dict(zip(halos, packs))

    terms = {}
    for h, moves in GATHERS:
        got = sent(with_halo[h], moves)
        for a, _ in moves:
            terms[a + 1] = (h, got)
    results = {1: terms.pop(1)}
    state, holder, late = results[1][1], None, 3
    for worker, steps in BLOCKS:
        first = steps[0]
        halo = PHASE_END[first] - first + 1
        if holder is None:
            pass
        elif PHASE_END[first] == PHASE_END[first - 1]:
            state = sent(state, [(holder, worker)])
        else:
            move = [(holder, worker)]
            parts = sent(edge, move, 1), sent(state, move), sent(edge, move, -1)
            (state,) = call(join_kernel, [(2 * EXT + TILE, *LAYER)], [], parts)
        waits = [held] if late in results and first == PHASE_END[late] + 1 else []
        for k in steps:
            halo = PHASE_END[k] - k + 1
            given, term = terms.get(k) or (halo - 1, with_halo[halo - 1])
            shapes = [(2 * (TILE + 2 * halo - 2) + TILE, *LAYER)]
            if halo == 1 and k < nt - 1:
                shapes.append((2 * TILE, *LAYER))
            state, *edge = call(
                functools.partial(coarse_kernel, halo, given, len(waits)), shapes, [], [state, tabs, term], waits=waits
            )
            edge = edge[0] if edge else None
            results[k] = (halo - 1, state)
            waits = []
            if k == late:
                (late_p,) = call(late_kernel, [(TILE, *LAYER)], [], [mine_p], waits=[state])
                relaxed, held = call(
                    relaxed_kernel, [whole, whole], [], [sent(late_p, ahead[:-1]), initial_state, kept, grown], place
                )
        holder = worker

    results[1] = (0, with_halo[0])
    received = []
    for sends in ROUNDS:
        plan = [(source, results[k][0]) for source, k, _ in sends]
        (payload,) = call(
            functools.partial(send_kernel, plan), [whole], [], [results[k][1] for _, k, _ in sends], place
        )
        received.append(sent(payload, [(source, target) for source, _, target in sends]))
    (corrected,) = call(
        functools.partial(
            corrected_kernel,
            [(device, results[k][0]) for device, k in KEPT],
            [[target for _, _, target in sends] for sends in ROUNDS],
        ),
        [whole],
        [],
        [held, *[results[k][1] for _, k in KEPT], *received],
        place,
    )
    return corrected[None], relaxed[None]


def solution(mesh):
    placed = (
        P(None, "space", None, None),
        P("tm", None, "space", None, None),
        P("space", None, None),
    )
    return jax.shard_map(
        functools.partial(on_device, mesh.shape["tm"], mesh.shape["space"]),
        mesh=mesh,
        in_specs=placed,
        out_specs=(P("tm", None, "space", None, None), P("tm", None, "space", None, None)),
        check_vma=False,
    )
```
